32 devices in a mesh: row: 8 (over z, core), col: 4 (over y, x).
Axes of the slice: x: 2, y: 2, z: 4, core: 2. Of those that a mesh axis runs over, the one named last changes fastest.
Arguments:
- inputs: bfloat16 [4096, 18432], P('col', 'row'), may hold values from -6 to 6
- out_grads: bfloat16 [4096, 18432], P('row', 'col'), may hold values from -0.09375 to 0.09375
- range_test: float32 [18432, 128], P('col'), may hold values from -0.046875 to 0.046875
- corange_test: float32 [256, 18432], P(None, 'row'), may hold values from -0.046875 to 0.046875
Outputs:
- range_sketch: float32 [18432, 128], P('row')
- corange_sketch: float32 [256, 18432], P(None, 'col')
- residual: float32 [18432, 18432], P('row', 'col')
The draws below stay inside these ranges and needn't reach their ends.
All inputs are finite; a program needn't handle non-finite values.
Results may differ from the reference program's by a relative error of at most 0.0003.
Values may be sent and summed in bfloat16 or wider, within the bound.
No kernel may reach another device: no remote copies, remote signals or barrier semaphores. Data moves between devices by JAX's collectives and lax.ppermute only.
A program may use at most 192 MiB of HBM per device.

```python
import jax
import jax.numpy as jnp
from jax import lax

M = 18432
N = 18432
RANK_Y = 128
RANK_Z = 256
TOKENS = 4096


def levels(stream_key, shape, cuts, low, largest):
    def one(axis_at, shards_of):
        steps = jax.random.uniform(jax.random.fold_in(jax.random.fold_in(stream_key, 6), axis_at), (shards_of,), jnp.float32, low / len(cuts), largest / len(cuts))
        return jnp.repeat(jnp.exp(steps), shape[axis_at] // shards_of).reshape((-1,) + (1,) * (len(shape) - axis_at - 1))

    factor_of = one(*cuts[0])
    for cut in cuts[1:]:
        factor_of = factor_of * one(*cut)
    return factor_of


def bell_draw(own_key, dims, scale, most, split=(), kind=jnp.bfloat16):
    factor_of = levels(own_key, dims, split, -0.22, 0.18) if split else 1.0
    array = jax.random.normal(own_key, dims, jnp.float32) * scale * factor_of
    return jnp.minimum(jnp.maximum(array, -most), most).astype(kind)


def setup_inputs(seed: int = 0) -> dict:
    arg_keys = jax.random.split(jax.random.key(seed), 5)
    return {
        "inputs": bell_draw(arg_keys[0], (TOKENS, M), 1.0, 6.0, ((0, 4), (1, 8))),
        "out_grads": bell_draw(arg_keys[1], (TOKENS, N), TOKENS ** -0.5, 0.09375, ((0, 8), (1, 4))),
        "range_test": bell_draw(arg_keys[2], (N, RANK_Y), N ** -0.5, 0.046875, ((0, 4),), jnp.float32),
        "corange_test": bell_draw(arg_keys[3], (RANK_Z, M), M ** -0.5, 0.046875, ((1, 8),), jnp.float32),
    }


def reference(inputs, out_grads, range_test, corange_test):
    highest = lax.Precision.HIGHEST
    gradient = lax.dot_general(inputs.astype(jnp.float32), out_grads.astype(jnp.float32), (((0,), (0,)), ((), ())), preferred_element_type=jnp.float32)
    range_sketch = jnp.dot(gradient.astype(jnp.float32), range_test.astype(jnp.float32), precision=highest, preferred_element_type=jnp.float32)
    corange_sketch = jnp.dot(corange_test.astype(jnp.float32), gradient.astype(jnp.float32), precision=highest, preferred_element_type=jnp.float32)
    core_input = jnp.dot(corange_test.astype(jnp.float32), range_sketch.astype(jnp.float32), precision=highest, preferred_element_type=jnp.float32)
    gram_matrix = jnp.dot(core_input.T.astype(jnp.float32), core_input.astype(jnp.float32), precision=highest, preferred_element_type=jnp.float32)
    factor_low = jnp.linalg.cholesky(gram_matrix)
    core_map = jax.scipy.linalg.cho_solve((factor_low, True), core_input.T)
    project = jnp.dot(core_map.astype(jnp.float32), corange_sketch.astype(jnp.float32), precision=highest, preferred_element_type=jnp.float32)
    residual = gradient - jnp.dot(range_sketch.astype(jnp.float32), project.astype(jnp.float32), precision=highest, preferred_element_type=jnp.float32)
    return (range_sketch, corange_sketch, residual)
```

```python
import math

import jax
import jax.numpy as jnp
from jax import lax
from jax.experimental import pallas as pl
from jax.experimental.pallas import tpu as pltpu
from jax.sharding import Mesh, PartitionSpec as P

highest = lax.Precision.HIGHEST
ROW = ("z", "core")
COL = ("a", "b")
VMEM_BYTES = 60 << 20


def exact_product(left, right, dims):
    return lax.dot_general(
        left, right, (dims, ((), ())), precision=highest, preferred_element_type=jnp.float32
    )


def split_two(array):
    high = array.astype(jnp.bfloat16)
    low = (array - high.astype(jnp.float32)).astype(jnp.bfloat16)
    return high, low


def largest_tile(size, limit):
    fits = [t for t in range(128, limit + 1, 128) if size % t == 0]
    return fits[-1] if fits else size


def shifted(array, axes, size, by):
    return lax.ppermute(array, axes, [(i, (i + by) % size) for i in range(size)])


def turn(array, after):
    rows, columns = array.shape
    half = rows // 2
    tile = largest_tile(columns, 384)

    def kernel(array_ref, *refs):
        refs[-2][...] = array_ref[:half, :].T
        refs[-1][...] = array_ref[half:, :].T

    return pl.pallas_call(
        kernel,
        grid=(columns // tile,),
        in_specs=[pl.BlockSpec((rows, tile), lambda i: (0, i))]
        + [pl.BlockSpec(memory_space=pl.ANY)] * len(after),
        out_specs=[pl.BlockSpec((tile, half), lambda i: (i, 0))] * 2,
        out_shape=[jax.ShapeDtypeStruct((columns, half), array.dtype)] * 2,
        compiler_params=pltpu.CompilerParams(vmem_limit_bytes=VMEM_BYTES),
    )(array, *after)


def gather_tokens(halves, sizes, index):
    near, far, near_starts, far_starts = [], [], [], []
    half = halves[0].shape[1]
    for part, start in enumerate(halves):
        order = (1, 0) if part == 0 else (0, 1)
        first, second = (COL[axis] for axis in order)
        size_first, size_second = (sizes[axis] for axis in order)

        def token(by_first, by_second):
            by = (by_second, by_first) if part == 0 else (by_first, by_second)
            at = [lax.rem(index[n] - by[n] + sizes[n], sizes[n]) for n in range(2)]
            return ((at[0] * sizes[1] + at[1]) * 2 + part) * half

        line = gathered_parts(start, first, size_first)
        near.append(line)
        near_starts += [token(by, 0) for by in range(size_first)]
        for by_second in range(1, size_second):
            far.append(shifted(line, second, size_second, by_second))
            far_starts += [token(by, by_second) for by in range(size_first)]
    return near, far, near_starts + far_starts


def scattered(parts, axes, size, index):
    terms = [lax.dynamic_index_in_dim(parts, index, 0, keepdims=False)]
    for by in range(1, size):
        target = lax.rem(index + by, size)
        sent = lax.dynamic_index_in_dim(parts, target, 0, keepdims=False)
        terms.append(shifted(sent, axes, size, by))
    return terms


def gathered_parts(own, axes, size):
    return jnp.concatenate([own] + [shifted(own, axes, size, by) for by in range(1, size)], axis=0)


def combine(left_terms, right_terms, after):
    count = len(left_terms)
    rank = left_terms[0].shape[1]
    unit, rank_z = right_terms[0].shape
    terms = list(left_terms) + list(right_terms)

    def kernel(*refs):
        ins, out_ref = refs[: len(terms)], refs[-1]
        left = ins[0][...]
        for ref in ins[1:count]:
            left += ref[...]
        right = ins[count][...]
        for ref in ins[count + 1 :]:
            right += ref[...]
        out_ref[:, :rank] = left
        out_ref[:, rank:] = right

    whole = pl.BlockSpec(memory_space=pltpu.VMEM)
    return pl.pallas_call(
        kernel,
        in_specs=[whole] * len(terms) + [pl.BlockSpec(memory_space=pl.ANY)] * len(after),
        out_specs=whole,
        out_shape=jax.ShapeDtypeStruct((unit, rank + rank_z), jnp.float32),
        compiler_params=pltpu.CompilerParams(vmem_limit_bytes=VMEM_BYTES),
    )(*terms, *after)


def finish(stacks, range_starts, test_starts, rank, after):
    rank_z = stacks[0].shape[1] - rank
    blocks = range_starts.shape[0] // len(stacks)
    tokens = stacks[0].shape[0] * len(stacks)
    unit = stacks[0].shape[0] // blocks
    step = largest_tile(tokens, 128)

    def kernel(range_starts_ref, test_starts_ref, *refs):
        ins = refs[: len(stacks)]
        parts_ref, high_ref, low_ref, core_ref, range_ref, test_ref = refs[-6:]
        for k, stack in enumerate(ins):

            @pl.loop(0, blocks)
            def _(i):
                rows = pl.ds(pl.multiple_of(i * unit, unit), unit)
                to = pl.multiple_of(range_starts_ref[k * blocks + i], unit)
                range_ref[pl.ds(to, unit), :] = stack[rows, :rank]
                to = pl.multiple_of(test_starts_ref[k * blocks + i], unit)
                test_ref[pl.ds(to, unit), :] = stack[rows, rank:]

        high, low = split_two(range_ref[...])
        parts_ref[:, :rank] = high
        parts_ref[:, rank:] = low
        for at in range(0, tokens, step):
            high, low = split_two(test_ref[at : at + step, :].T)
            high_ref[:, at : at + step] = high
            low_ref[:, at : at + step] = low
        core_ref[...] = lax.dot_general(
            test_ref[...],
            range_ref[...],
            (((0,), (0,)), ((), ())),
            precision=highest,
            preferred_element_type=jnp.float32,
        )

    whole = pl.BlockSpec(memory_space=pltpu.VMEM)
    return pl.pallas_call(
        kernel,
        grid_spec=pltpu.PrefetchScalarGridSpec(
            num_scalar_prefetch=2,
            grid=(),
            in_specs=[whole] * len(stacks) + [pl.BlockSpec(memory_space=pl.ANY)] * len(after),
            out_specs=[whole] * 4,
            scratch_shapes=[
                pltpu.VMEM((tokens, rank), jnp.float32),
                pltpu.VMEM((tokens, rank_z), jnp.float32),
            ],
        ),
        out_shape=[
            jax.ShapeDtypeStruct((tokens, 2 * rank), jnp.bfloat16),
            jax.ShapeDtypeStruct((rank_z, tokens), jnp.bfloat16),
            jax.ShapeDtypeStruct((rank_z, tokens), jnp.bfloat16),
            jax.ShapeDtypeStruct((rank_z, rank), jnp.float32),
        ],
        compiler_params=pltpu.CompilerParams(vmem_limit_bytes=VMEM_BYTES),
    )(range_starts, test_starts, *stacks, *after)


def assemble(stacks, starts, test_parts):
    starts = jnp.stack(starts).astype(jnp.int32)
    width = stacks[0].shape[1]
    tokens = test_parts.shape[0]
    rows = sum(stack.shape[0] for stack in stacks) * width // tokens
    rank = test_parts.shape[1] // 2
    tile = largest_tile(rows, 384)
    arrays, specs = [], []
    for stack in stacks:
        for place in range(stack.shape[0] // rows):
            first = place * (rows // tile)
            arrays.append(stack)
            specs.append(pl.BlockSpec((tile, width), lambda i, s, first=first: (first + i, 0)))

    def kernel(starts_ref, *refs):
        ins, test_ref = refs[: len(arrays)], refs[len(arrays)]
        all_ref, sketch_ref, split_ref = refs[-3:]
        for k, piece in enumerate(ins):
            all_ref[:, pl.ds(pl.multiple_of(starts_ref[k], width), width)] = piece[...]
        both = jnp.dot(all_ref[...], test_ref[...], preferred_element_type=jnp.float32)
        sketch = both[:, :rank] + both[:, rank:]
        sketch_ref[...] = sketch
        high, low = split_two(sketch)
        split_ref[:, :rank] = high
        split_ref[:, rank : 2 * rank] = low
        split_ref[:, 2 * rank :] = high

    return pl.pallas_call(
        kernel,
        grid_spec=pltpu.PrefetchScalarGridSpec(
            num_scalar_prefetch=1,
            grid=(rows // tile,),
            in_specs=specs + [pl.BlockSpec((tokens, 2 * rank), lambda i, s: (0, 0))],
            out_specs=[
                pl.BlockSpec((tile, tokens), lambda i, s: (i, 0)),
                pl.BlockSpec((tile, rank), lambda i, s: (i, 0)),
                pl.BlockSpec((tile, 3 * rank), lambda i, s: (i, 0)),
            ],
        ),
        out_shape=[
            jax.ShapeDtypeStruct((rows, tokens), jnp.bfloat16),
            jax.ShapeDtypeStruct((rows, rank), jnp.float32),
            jax.ShapeDtypeStruct((rows, 3 * rank), jnp.bfloat16),
        ],
        compiler_params=pltpu.CompilerParams(vmem_limit_bytes=VMEM_BYTES),
        cost_estimate=pl.CostEstimate(
            flops=4 * rows * tokens * rank, bytes_accessed=4 * rows * tokens, transcendentals=0
        ),
    )(starts, *arrays, test_parts)


def slab(rows_all, grads, sketch_split, test_high, test_low, core_map, first, block, columns, before):
    rows, tokens = rows_all.shape
    width = grads.shape[1]
    rank, rank_z = core_map.shape
    tile = largest_tile(rows, 768)
    at = first // block

    def kernel(rows_ref, grads_ref, split_ref, high_ref, low_ref, map_ref, *refs):
        corange_ref, residual_ref, project_ref = refs[-3:]

        @pl.when(pl.program_id(1) == 0)
        def _():
            corange = jnp.dot(high_ref[...], grads_ref[...], preferred_element_type=jnp.float32)
            corange += jnp.dot(low_ref[...], grads_ref[...], preferred_element_type=jnp.float32)
            corange_ref[...] = corange
            project = -jnp.dot(
                map_ref[...], corange, precision=highest, preferred_element_type=jnp.float32
            )
            high, low = split_two(project)
            project_ref[:rank, :] = high
            project_ref[rank : 2 * rank, :] = high
            project_ref[2 * rank :, :] = low

        residual_ref[...] = jnp.dot(
            rows_ref[...], grads_ref[...], preferred_element_type=jnp.float32
        ) + jnp.dot(split_ref[...], project_ref[...], preferred_element_type=jnp.float32)

    in_specs = [
        pl.BlockSpec((tile, tokens), lambda j, i: (i, 0)),
        pl.BlockSpec((tokens, block), lambda j, i: (0, j)),
        pl.BlockSpec((tile, 3 * rank), lambda j, i: (i, 0)),
        pl.BlockSpec((rank_z, tokens), lambda j, i: (0, 0)),
        pl.BlockSpec((rank_z, tokens), lambda j, i: (0, 0)),
        pl.BlockSpec((rank, rank_z), lambda j, i: (0, 0)),
    ] + [pl.BlockSpec(memory_space=pl.ANY)] * len(before)
    return pl.pallas_call(
        kernel,
        grid=(width // block, rows // tile),
        in_specs=in_specs,
        out_specs=[
            pl.BlockSpec((rank_z, block), lambda j, i: (0, at + j)),
            pl.BlockSpec((tile, block), lambda j, i: (i, at + j)),
        ],
        out_shape=[
            jax.ShapeDtypeStruct((rank_z, columns), jnp.float32),
            jax.ShapeDtypeStruct((rows, columns), jnp.float32),
        ],
        scratch_shapes=[pltpu.VMEM((3 * rank, block), jnp.bfloat16)],
        input_output_aliases={6: 0, 7: 1} if before else {},
        compiler_params=pltpu.CompilerParams(vmem_limit_bytes=VMEM_BYTES),
        cost_estimate=pl.CostEstimate(
            flops=2 * width * (rows * (tokens + 3 * rank) + 2 * rank_z * tokens),
            bytes_accessed=4 * rows * width + 2 * tokens * (rows + width),
            transcendentals=0,
        ),
    )(rows_all, grads, sketch_split, test_high, test_low, core_map, *before)


def slices_of(columns):
    unit = largest_tile(columns, 512)
    count = columns // unit
    last = max(1, count // 9)
    middle = max(1, 2 * count // 9)
    slices, first = [], 0
    for n in (count - middle - last, middle, last):
        if n > 0:
            twice = n % 2 == 0 and first % (2 * unit) == 0
            slices.append((first, n * unit, 2 * unit if twice else unit))
            first += n * unit
    return slices


def solution(mesh):
    size_row, size_col = mesh.shape["row"], mesh.shape["col"]
    size_b = next(n for n in range(math.isqrt(size_col), size_col + 1) if size_col % n == 0)
    size_a = size_col // size_b
    size_core = 2 if size_row % 2 == 0 else 1
    size_z = size_row // size_core
    finer = Mesh(mesh.devices.reshape(size_z, size_core, size_a, size_b), ROW + COL)

    def per_device(inputs, out_grads, range_test, corange_test):
        z, core = lax.axis_index("z"), lax.axis_index("core")
        a, b = lax.axis_index("a"), lax.axis_index("b")
        col = a * size_b + b
        columns = out_grads.shape[1]
        rank, rank_z = range_test.shape[1], corange_test.shape[0]

        gathered = []
        for first, width, block in slices_of(columns):
            part = out_grads[:, first : first + width]
            gathered.append((first, block, lax.all_gather(part, ROW, axis=0, tiled=True)))

        grads_range = exact_product(out_grads.astype(jnp.float32), range_test, ((1,), (0,)))
        test_inputs = exact_product(inputs.astype(jnp.float32), corange_test, ((1,), (1,)))
        tokens = inputs.shape[0] * size_col
        unit = inputs.shape[0] // size_row
        range_terms = scattered(grads_range.reshape(size_col, unit, rank), COL, size_col, col)
        halves = turn(inputs, range_terms)
        near, far, starts = gather_tokens(halves, (size_a, size_b), (a, b))
        test_inputs = test_inputs.reshape(size_z, size_core, unit, rank_z).transpose(1, 0, 2, 3)
        test_inputs = sum(scattered(test_inputs, "core", size_core, core))
        test_terms = scattered(test_inputs, "z", size_z, z)
        own = combine(range_terms, test_terms, near)
        own = gathered_parts(own, "z", size_z)
        own = gathered_parts(own, COL, size_col)
        stacks = [own] + [shifted(own, "core", size_core, by) for by in range(1, size_core)]
        at_core = lax.rem(core - jnp.arange(size_core) + size_core, size_core)[:, None, None]
        at_col = lax.rem(col - jnp.arange(size_col) + size_col, size_col)[None, :, None]
        at_z = lax.rem(z - jnp.arange(size_z) + size_z, size_z)[None, None, :]
        at_row = at_z * size_core + at_core
        range_starts = (at_row * size_col + at_col) * unit
        test_starts = (at_col * size_row + at_row) * unit
        range_parts, test_high, test_low, core_input = finish(
            stacks,
            range_starts.reshape(-1).astype(jnp.int32),
            test_starts.reshape(-1).astype(jnp.int32),
            rank,
            [],
        )

        gram_matrix = exact_product(core_input, core_input, ((0,), (0,)))
        factor_low = jnp.linalg.cholesky(gram_matrix)
        core_map = jax.scipy.linalg.cho_solve((factor_low, True), core_input.T)

        rows_all, new_range, sketch_split = assemble(near + far, starts, range_parts)

        out = ()
        for first, block, grads in gathered:
            out = slab(
                rows_all, grads, sketch_split, test_high, test_low, core_map, first, block, columns, out
            )
        return (new_range, out[0], out[1])

    return jax.shard_map(
        per_device,
        mesh=finer,
        in_specs=(P(COL, ROW), P(ROW, COL), P(COL, None), P(None, ROW)),
        out_specs=(P(ROW, None), P(None, COL), P(ROW, COL)),
        check_vma=False,
    )
```

```python
import math

import jax
import jax.numpy as jnp
from jax import lax
from jax.experimental import pallas as pl
from jax.experimental.pallas import tpu as pltpu
from jax.sharding import Mesh, PartitionSpec as P

highest = lax.Precision.HIGHEST
ROW = ("z", "core")
COL = ("a", "b")
VMEM_BYTES = 60 << 20


def exact_product(left, right, dims):
    return lax.dot_general(
        left, right, (dims, ((), ())), precision=highest, preferred_element_type=jnp.float32
    )


def split_two(array):
    high = array.astype(jnp.bfloat16)
    low = (array - high.astype(jnp.float32)).astype(jnp.bfloat16)
    return high, low


def largest_tile(size, limit):
    fits = [t for t in range(128, limit + 1, 128) if size % t == 0]
    return fits[-1] if fits else size


def shifted(array, axes, size, by):
    return lax.ppermute(array, axes, [(i, (i + by) % size) for i in range(size)])


def turn(array, after):
    rows, columns = array.shape
    half = rows // 2
    tile = largest_tile(columns, 384)

    def kernel(array_ref, *refs):
        refs[-2][...] = array_ref[:half, :].T
        refs[-1][...] = array_ref[half:, :].T

    return pl.pallas_call(
        kernel,
        grid=(columns // tile,),
        in_specs=[pl.BlockSpec((rows, tile), lambda i: (0, i))]
        + [pl.BlockSpec(memory_space=pl.ANY)] * len(after),
        out_specs=[pl.BlockSpec((tile, half), lambda i: (i, 0))] * 2,
        out_shape=[jax.ShapeDtypeStruct((columns, half), array.dtype)] * 2,
        compiler_params=pltpu.CompilerParams(vmem_limit_bytes=VMEM_BYTES),
    )(array, *after)


def gather_tokens(halves, sizes, index):
    rounds, starts = ([], [], []), ([], [], [])
    half = halves[0].shape[1]
    for part, start in enumerate(halves):
        order = (1, 0) if part == 0 else (0, 1)
        first, second = (COL[axis] for axis in order)
        size_first, size_second = (sizes[axis] for axis in order)

        def add(place, piece, by_first, by_second):
            by = (by_second, by_first) if part == 0 else (by_first, by_second)
            at = [lax.rem(index[n] - by[n] + sizes[n], sizes[n]) for n in range(2)]
            rounds[place].append(piece)
            starts[place].append(((at[0] * sizes[1] + at[1]) * 2 + part) * half)

        add(0, start, 0, 0)
        line = [start] + [shifted(start, first, size_first, by) for by in range(1, size_first)]
        for by in range(1, size_first):
            add(0, line[by], by, 0)
        for by_second in range(1, size_second):
            for by in range(size_first):
                piece = shifted(line[by], second, size_second, by_second)
                add(1 if by == 0 else 2, piece, by, by_second)
    return rounds, sum(starts, [])


def scattered(parts, axes, size, index):
    terms = [lax.dynamic_index_in_dim(parts, index, 0, keepdims=False)]
    for by in range(1, size):
        target = lax.rem(index + by, size)
        sent = lax.dynamic_index_in_dim(parts, target, 0, keepdims=False)
        terms.append(shifted(sent, axes, size, by))
    return terms


def gathered_parts(own, axes, size):
    return jnp.concatenate([own] + [shifted(own, axes, size, by) for by in range(1, size)], axis=0)


def below(terms, after):
    rows, columns = terms[0].shape

    def kernel(*refs):
        for k in range(len(terms)):
            refs[-1][k * rows : (k + 1) * rows, :] = refs[k][...]

    whole = pl.BlockSpec(memory_space=pltpu.VMEM)
    return pl.pallas_call(
        kernel,
        in_specs=[whole] * len(terms) + [pl.BlockSpec(memory_space=pl.ANY)] * len(after),
        out_specs=whole,
        out_shape=jax.ShapeDtypeStruct((len(terms) * rows, columns), terms[0].dtype),
        compiler_params=pltpu.CompilerParams(vmem_limit_bytes=VMEM_BYTES),
    )(*terms, *after)


def combine(left_terms, right_terms, after):
    count = len(left_terms)
    rank = left_terms[0].shape[1]
    unit, rank_z = right_terms[0].shape
    terms = list(left_terms) + list(right_terms)

    def kernel(*refs):
        ins, out_ref = refs[: len(terms)], refs[-1]
        left = ins[0][...]
        for ref in ins[1:count]:
            left += ref[...]
        right = ins[count][...]
        for ref in ins[count + 1 :]:
            right += ref[...]
        out_ref[:, :rank] = left
        out_ref[:, rank:] = right

    whole = pl.BlockSpec(memory_space=pltpu.VMEM)
    return pl.pallas_call(
        kernel,
        in_specs=[whole] * len(terms) + [pl.BlockSpec(memory_space=pl.ANY)] * len(after),
        out_specs=whole,
        out_shape=jax.ShapeDtypeStruct((unit, rank + rank_z), jnp.float32),
        compiler_params=pltpu.CompilerParams(vmem_limit_bytes=VMEM_BYTES),
    )(*terms, *after)


def finish(stacks, range_starts, test_starts, rank):
    rank_z = stacks[0].shape[1] - rank
    blocks = range_starts.shape[0] // len(stacks)
    tokens = stacks[0].shape[0] * len(stacks)
    unit = stacks[0].shape[0] // blocks
    step = largest_tile(tokens, 128)

    def kernel(range_starts_ref, test_starts_ref, *refs):
        ins = refs[: len(stacks)]
        parts_ref, high_ref, low_ref, core_ref, range_ref, test_ref = refs[-6:]
        for k, stack in enumerate(ins):

            @pl.loop(0, blocks)
            def _(i):
                rows = pl.ds(pl.multiple_of(i * unit, unit), unit)
                to = pl.multiple_of(range_starts_ref[k * blocks + i], unit)
                range_ref[pl.ds(to, unit), :] = stack[rows, :rank]
                to = pl.multiple_of(test_starts_ref[k * blocks + i], unit)
                test_ref[pl.ds(to, unit), :] = stack[rows, rank:]

        high, low = split_two(range_ref[...])
        parts_ref[:, :rank] = high
        parts_ref[:, rank:] = low
        for at in range(0, tokens, step):
            high, low = split_two(test_ref[at : at + step, :].T)
            high_ref[:, at : at + step] = high
            low_ref[:, at : at + step] = low
        core_ref[...] = lax.dot_general(
            test_ref[...],
            range_ref[...],
            (((0,), (0,)), ((), ())),
            precision=highest,
            preferred_element_type=jnp.float32,
        )

    whole = pl.BlockSpec(memory_space=pltpu.VMEM)
    return pl.pallas_call(
        kernel,
        grid_spec=pltpu.PrefetchScalarGridSpec(
            num_scalar_prefetch=2,
            grid=(),
            in_specs=[whole] * len(stacks),
            out_specs=[whole] * 4,
            scratch_shapes=[
                pltpu.VMEM((tokens, rank), jnp.float32),
                pltpu.VMEM((tokens, rank_z), jnp.float32),
            ],
        ),
        out_shape=[
            jax.ShapeDtypeStruct((tokens, 2 * rank), jnp.bfloat16),
            jax.ShapeDtypeStruct((rank_z, tokens), jnp.bfloat16),
            jax.ShapeDtypeStruct((rank_z, tokens), jnp.bfloat16),
            jax.ShapeDtypeStruct((rank_z, rank), jnp.float32),
        ],
        compiler_params=pltpu.CompilerParams(vmem_limit_bytes=VMEM_BYTES),
    )(range_starts, test_starts, *stacks)


def assemble(stacks, starts, test_parts):
    starts = jnp.stack(starts).astype(jnp.int32)
    width = stacks[0].shape[1]
    tokens = test_parts.shape[0]
    rows = sum(stack.shape[0] for stack in stacks) * width // tokens
    rank = test_parts.shape[1] // 2
    tile = largest_tile(rows, 384)
    arrays, specs = [], []
    for stack in stacks:
        for place in range(stack.shape[0] // rows):
            first = place * (rows // tile)
            arrays.append(stack)
            specs.append(pl.BlockSpec((tile, width), lambda i, s, first=first: (first + i, 0)))

    def kernel(starts_ref, *refs):
        ins, test_ref = refs[: len(arrays)], refs[len(arrays)]
        all_ref, sketch_ref, split_ref = refs[-3:]
        for k, piece in enumerate(ins):
            all_ref[:, pl.ds(pl.multiple_of(starts_ref[k], width), width)] = piece[...]
        both = jnp.dot(all_ref[...], test_ref[...], preferred_element_type=jnp.float32)
        sketch = both[:, :rank] + both[:, rank:]
        sketch_ref[...] = sketch
        high, low = split_two(sketch)
        split_ref[:, :rank] = high
        split_ref[:, rank : 2 * rank] = low
        split_ref[:, 2 * rank :] = high

    return pl.pallas_call(
        kernel,
        grid_spec=pltpu.PrefetchScalarGridSpec(
            num_scalar_prefetch=1,
            grid=(rows // tile,),
            in_specs=specs + [pl.BlockSpec((tokens, 2 * rank), lambda i, s: (0, 0))],
            out_specs=[
                pl.BlockSpec((tile, tokens), lambda i, s: (i, 0)),
                pl.BlockSpec((tile, rank), lambda i, s: (i, 0)),
                pl.BlockSpec((tile, 3 * rank), lambda i, s: (i, 0)),
            ],
        ),
        out_shape=[
            jax.ShapeDtypeStruct((rows, tokens), jnp.bfloat16),
            jax.ShapeDtypeStruct((rows, rank), jnp.float32),
            jax.ShapeDtypeStruct((rows, 3 * rank), jnp.bfloat16),
        ],
        compiler_params=pltpu.CompilerParams(vmem_limit_bytes=VMEM_BYTES),
        cost_estimate=pl.CostEstimate(
            flops=4 * rows * tokens * rank, bytes_accessed=4 * rows * tokens, transcendentals=0
        ),
    )(starts, *arrays, test_parts)


def slab(rows_all, grads, sketch_split, test_high, test_low, core_map, first, block, columns, before):
    rows, tokens = rows_all.shape
    width = grads.shape[1]
    rank, rank_z = core_map.shape
    tile = largest_tile(rows, 768)
    at = first // block

    def kernel(rows_ref, grads_ref, split_ref, high_ref, low_ref, map_ref, *refs):
        corange_ref, residual_ref, project_ref = refs[-3:]

        @pl.when(pl.program_id(1) == 0)
        def _():
            corange = jnp.dot(high_ref[...], grads_ref[...], preferred_element_type=jnp.float32)
            corange += jnp.dot(low_ref[...], grads_ref[...], preferred_element_type=jnp.float32)
            corange_ref[...] = corange
            project = -jnp.dot(
                map_ref[...], corange, precision=highest, preferred_element_type=jnp.float32
            )
            high, low = split_two(project)
            project_ref[:rank, :] = high
            project_ref[rank : 2 * rank, :] = high
            project_ref[2 * rank :, :] = low

        residual_ref[...] = jnp.dot(
            rows_ref[...], grads_ref[...], preferred_element_type=jnp.float32
        ) + jnp.dot(split_ref[...], project_ref[...], preferred_element_type=jnp.float32)

    in_specs = [
        pl.BlockSpec((tile, tokens), lambda j, i: (i, 0)),
        pl.BlockSpec((tokens, block), lambda j, i: (0, j)),
        pl.BlockSpec((tile, 3 * rank), lambda j, i: (i, 0)),
        pl.BlockSpec((rank_z, tokens), lambda j, i: (0, 0)),
        pl.BlockSpec((rank_z, tokens), lambda j, i: (0, 0)),
        pl.BlockSpec((rank, rank_z), lambda j, i: (0, 0)),
    ] + [pl.BlockSpec(memory_space=pl.ANY)] * len(before)
    return pl.pallas_call(
        kernel,
        grid=(width // block, rows // tile),
        in_specs=in_specs,
        out_specs=[
            pl.BlockSpec((rank_z, block), lambda j, i: (0, at + j)),
            pl.BlockSpec((tile, block), lambda j, i: (i, at + j)),
        ],
        out_shape=[
            jax.ShapeDtypeStruct((rank_z, columns), jnp.float32),
            jax.ShapeDtypeStruct((rows, columns), jnp.float32),
        ],
        scratch_shapes=[pltpu.VMEM((3 * rank, block), jnp.bfloat16)],
        input_output_aliases={6: 0, 7: 1} if before else {},
        compiler_params=pltpu.CompilerParams(vmem_limit_bytes=VMEM_BYTES),
        cost_estimate=pl.CostEstimate(
            flops=2 * width * (rows * (tokens + 3 * rank) + 2 * rank_z * tokens),
            bytes_accessed=4 * rows * width + 2 * tokens * (rows + width),
            transcendentals=0,
        ),
    )(rows_all, grads, sketch_split, test_high, test_low, core_map, *before)


def slices_of(columns):
    unit = largest_tile(columns, 512)
    count = columns // unit
    last = max(1, count // 9)
    middle = max(1, 2 * count // 9)
    slices, first = [], 0
    for n in (count - middle - last, middle, last):
        if n > 0:
            twice = n % 2 == 0 and first % (2 * unit) == 0
            slices.append((first, n * unit, 2 * unit if twice else unit))
            first += n * unit
    return slices


def solution(mesh):
    size_row, size_col = mesh.shape["row"], mesh.shape["col"]
    size_b = next(n for n in range(math.isqrt(size_col), size_col + 1) if size_col % n == 0)
    size_a = size_col // size_b
    size_core = 2 if size_row % 2 == 0 else 1
    size_z = size_row // size_core
    finer = Mesh(mesh.devices.reshape(size_z, size_core, size_a, size_b), ROW + COL)

    def per_device(inputs, out_grads, range_test, corange_test):
        z, core = lax.axis_index("z"), lax.axis_index("core")
        a, b = lax.axis_index("a"), lax.axis_index("b")
        col = a * size_b + b
        columns = out_grads.shape[1]
        rank, rank_z = range_test.shape[1], corange_test.shape[0]

        gathered = []
        for first, width, block in slices_of(columns):
            part = out_grads[:, first : first + width]
            gathered.append((first, block, lax.all_gather(part, ROW, axis=0, tiled=True)))

        grads_range = exact_product(out_grads.astype(jnp.float32), range_test, ((1,), (0,)))
        test_inputs = exact_product(inputs.astype(jnp.float32), corange_test, ((1,), (1,)))
        tokens = inputs.shape[0] * size_col
        unit = inputs.shape[0] // size_row
        range_terms = scattered(grads_range.reshape(size_col, unit, rank), COL, size_col, col)
        halves = turn(inputs, range_terms)
        rounds, starts = gather_tokens(halves, (size_a, size_b), (a, b))
        test_inputs = test_inputs.reshape(size_z, size_core, unit, rank_z).transpose(1, 0, 2, 3)
        test_inputs = sum(scattered(test_inputs, "core", size_core, core))
        test_terms = scattered(test_inputs, "z", size_z, z)
        own = combine(range_terms, test_terms, rounds[0])
        own = below([own] + [shifted(own, "z", size_z, by) for by in range(1, size_z)], rounds[1])
        own = gathered_parts(own, COL, size_col)
        stacks = [own] + [shifted(own, "core", size_core, by) for by in range(1, size_core)]
        at_core = lax.rem(core - jnp.arange(size_core) + size_core, size_core)[:, None, None]
        at_col = lax.rem(col - jnp.arange(size_col) + size_col, size_col)[None, :, None]
        at_z = lax.rem(z - jnp.arange(size_z) + size_z, size_z)[None, None, :]
        at_row = at_z * size_core + at_core
        range_starts = (at_row * size_col + at_col) * unit
        test_starts = (at_col * size_row + at_row) * unit
        range_parts, test_high, test_low, core_input = finish(
            stacks,
            range_starts.reshape(-1).astype(jnp.int32),
            test_starts.reshape(-1).astype(jnp.int32),
            rank,
        )

        gram_matrix = exact_product(core_input, core_input, ((0,), (0,)))
        factor_low = jnp.linalg.cholesky(gram_matrix)
        core_map = jax.scipy.linalg.cho_solve((factor_low, True), core_input.T)

        rows_all, new_range, sketch_split = assemble(sum(rounds, []), starts, range_parts)

        out = ()
        for first, block, grads in gathered:
            out = slab(
                rows_all, grads, sketch_split, test_high, test_low, core_map, first, block, columns, out
            )
        return (new_range, out[0], out[1])

    return jax.shard_map(
        per_device,
        mesh=finer,
        in_specs=(P(COL, ROW), P(ROW, COL), P(COL, None), P(None, ROW)),
        out_specs=(P(ROW, None), P(None, COL), P(ROW, COL)),
        check_vma=False,
    )
```

```python
import math

import jax
import jax.numpy as jnp
from jax import lax
from jax.experimental import pallas as pl
from jax.experimental.pallas import tpu as pltpu
from jax.sharding import Mesh, PartitionSpec as P

highest = lax.Precision.HIGHEST
ROW = ("z", "core")
COL = ("a", "b")
VMEM_BYTES = 60 << 20


def exact_product(left, right, dims):
    return lax.dot_general(
        left, right, (dims, ((), ())), precision=highest, preferred_element_type=jnp.float32
    )


def split_two(array):
    high = array.astype(jnp.bfloat16)
    low = (array - high.astype(jnp.float32)).astype(jnp.bfloat16)
    return high, low


def largest_tile(size, limit):
    fits = [t for t in range(128, limit + 1, 128) if size % t == 0]
    return fits[-1] if fits else size


def shifted(array, axes, size, by):
    return lax.ppermute(array, axes, [(i, (i + by) % size) for i in range(size)])


def turn(array, after):
    rows, columns = array.shape
    half = rows // 2
    tile = largest_tile(columns, 384)

    def kernel(array_ref, *refs):
        refs[-2][...] = array_ref[:half, :].T
        refs[-1][...] = array_ref[half:, :].T

    return pl.pallas_call(
        kernel,
        grid=(columns // tile,),
        in_specs=[pl.BlockSpec((rows, tile), lambda i: (0, i))]
        + [pl.BlockSpec(memory_space=pl.ANY)] * len(after),
        out_specs=[pl.BlockSpec((tile, half), lambda i: (i, 0))] * 2,
        out_shape=[jax.ShapeDtypeStruct((columns, half), array.dtype)] * 2,
        compiler_params=pltpu.CompilerParams(vmem_limit_bytes=VMEM_BYTES),
    )(array, *after)


def gather_tokens(halves, sizes, index):
    rounds, starts = ([], [], []), ([], [], [])
    half = halves[0].shape[1]
    for part, start in enumerate(halves):
        order = (1, 0) if part == 0 else (0, 1)
        first, second = (COL[axis] for axis in order)
        size_first, size_second = (sizes[axis] for axis in order)

        def add(place, piece, by_first, by_second):
            by = (by_second, by_first) if part == 0 else (by_first, by_second)
            at = [lax.rem(index[n] - by[n] + sizes[n], sizes[n]) for n in range(2)]
            rounds[place].append(piece)
            starts[place].append(((at[0] * sizes[1] + at[1]) * 2 + part) * half)

        add(0, start, 0, 0)
        line = [start] + [shifted(start, first, size_first, by) for by in range(1, size_first)]
        for by in range(1, size_first):
            add(0, line[by], by, 0)
        for by_second in range(1, size_second):
            for by in range(size_first):
                piece = shifted(line[by], second, size_second, by_second)
                add(1 if by == 0 else 2, piece, by, by_second)
    return rounds, sum(starts, [])


def scattered(parts, axes, size, index):
    terms = [lax.dynamic_index_in_dim(parts, index, 0, keepdims=False)]
    for by in range(1, size):
        target = lax.rem(index + by, size)
        sent = lax.dynamic_index_in_dim(parts, target, 0, keepdims=False)
        terms.append(shifted(sent, axes, size, by))
    return terms


def gathered_parts(own, axes, size):
    return jnp.concatenate([own] + [shifted(own, axes, size, by) for by in range(1, size)], axis=0)


def below(terms, after):
    rows, columns = terms[0].shape

    def kernel(*refs):
        for k in range(len(terms)):
            refs[-1][k * rows : (k + 1) * rows, :] = refs[k][...]

    whole = pl.BlockSpec(memory_space=pltpu.VMEM)
    return pl.pallas_call(
        kernel,
        in_specs=[whole] * len(terms) + [pl.BlockSpec(memory_space=pl.ANY)] * len(after),
        out_specs=whole,
        out_shape=jax.ShapeDtypeStruct((len(terms) * rows, columns), terms[0].dtype),
        compiler_params=pltpu.CompilerParams(vmem_limit_bytes=VMEM_BYTES),
    )(*terms, *after)


def combine(left_terms, right_terms, after):
    count = len(left_terms)
    rank = left_terms[0].shape[1]
    unit, rank_z = right_terms[0].shape
    terms = list(left_terms) + list(right_terms)

    def kernel(*refs):
        ins, out_ref = refs[: len(terms)], refs[-1]
        left = ins[0][...]
        for ref in ins[1:count]:
            left += ref[...]
        right = ins[count][...]
        for ref in ins[count + 1 :]:
            right += ref[...]
        out_ref[:, :rank] = left
        out_ref[:, rank:] = right

    whole = pl.BlockSpec(memory_space=pltpu.VMEM)
    return pl.pallas_call(
        kernel,
        in_specs=[whole] * len(terms) + [pl.BlockSpec(memory_space=pl.ANY)] * len(after),
        out_specs=whole,
        out_shape=jax.ShapeDtypeStruct((unit, rank + rank_z), jnp.float32),
        compiler_params=pltpu.CompilerParams(vmem_limit_bytes=VMEM_BYTES),
    )(*terms, *after)


def finish(stacks, range_starts, test_starts, rank):
    rank_z = stacks[0].shape[1] - rank
    blocks = range_starts.shape[0] // len(stacks)
    tokens = stacks[0].shape[0] * len(stacks)
    unit = stacks[0].shape[0] // blocks
    step = largest_tile(tokens, 128)

    def kernel(range_starts_ref, test_starts_ref, *refs):
        ins = refs[: len(stacks)]
        parts_ref, high_ref, low_ref, core_ref, range_ref, test_ref = refs[-6:]
        for k, stack in enumerate(ins):

            @pl.loop(0, blocks)
            def _(i):
                rows = pl.ds(pl.multiple_of(i * unit, unit), unit)
                to = pl.multiple_of(range_starts_ref[k * blocks + i], unit)
                range_ref[pl.ds(to, unit), :] = stack[rows, :rank]
                to = pl.multiple_of(test_starts_ref[k * blocks + i], unit)
                test_ref[pl.ds(to, unit), :] = stack[rows, rank:]

        high, low = split_two(range_ref[...])
        parts_ref[:, :rank] = high
        parts_ref[:, rank:] = low
        for at in range(0, tokens, step):
            high, low = split_two(test_ref[at : at + step, :].T)
            high_ref[:, at : at + step] = high
            low_ref[:, at : at + step] = low
        core_ref[...] = lax.dot_general(
            test_ref[...],
            range_ref[...],
            (((0,), (0,)), ((), ())),
            precision=highest,
            preferred_element_type=jnp.float32,
        )

    whole = pl.BlockSpec(memory_space=pltpu.VMEM)
    return pl.pallas_call(
        kernel,
        grid_spec=pltpu.PrefetchScalarGridSpec(
            num_scalar_prefetch=2,
            grid=(),
            in_specs=[whole] * len(stacks),
            out_specs=[whole] * 4,
            scratch_shapes=[
                pltpu.VMEM((tokens, rank), jnp.float32),
                pltpu.VMEM((tokens, rank_z), jnp.float32),
            ],
        ),
        out_shape=[
            jax.ShapeDtypeStruct((tokens, 2 * rank), jnp.bfloat16),
            jax.ShapeDtypeStruct((rank_z, tokens), jnp.bfloat16),
            jax.ShapeDtypeStruct((rank_z, tokens), jnp.bfloat16),
            jax.ShapeDtypeStruct((rank_z, rank), jnp.float32),
        ],
        compiler_params=pltpu.CompilerParams(vmem_limit_bytes=VMEM_BYTES),
    )(range_starts, test_starts, *stacks)


def assemble(stacks, starts, test_parts):
    starts = jnp.stack(starts).astype(jnp.int32)
    width = stacks[0].shape[1]
    tokens = test_parts.shape[0]
    rows = sum(stack.shape[0] for stack in stacks) * width // tokens
    rank = test_parts.shape[1] // 2
    tile = largest_tile(rows, 384)
    arrays, specs = [], []
    for stack in stacks:
        for place in range(stack.shape[0] // rows):
            first = place * (rows // tile)
            arrays.append(stack)
            specs.append(pl.BlockSpec((tile, width), lambda i, s, first=first: (first + i, 0)))

    def kernel(starts_ref, *refs):
        ins, test_ref = refs[: len(arrays)], refs[len(arrays)]
        all_ref, sketch_ref, split_ref = refs[-3:]
        for k, piece in enumerate(ins):
            all_ref[:, pl.ds(pl.multiple_of(starts_ref[k], width), width)] = piece[...]
        both = jnp.dot(all_ref[...], test_ref[...], preferred_element_type=jnp.float32)
        sketch = both[:, :rank] + both[:, rank:]
        sketch_ref[...] = sketch
        high, low = split_two(sketch)
        split_ref[:, :rank] = high
        split_ref[:, rank : 2 * rank] = low
        split_ref[:, 2 * rank :] = high

    return pl.pallas_call(
        kernel,
        grid_spec=pltpu.PrefetchScalarGridSpec(
            num_scalar_prefetch=1,
            grid=(rows // tile,),
            in_specs=specs + [pl.BlockSpec((tokens, 2 * rank), lambda i, s: (0, 0))],
            out_specs=[
                pl.BlockSpec((tile, tokens), lambda i, s: (i, 0)),
                pl.BlockSpec((tile, rank), lambda i, s: (i, 0)),
                pl.BlockSpec((tile, 3 * rank), lambda i, s: (i, 0)),
            ],
        ),
        out_shape=[
            jax.ShapeDtypeStruct((rows, tokens), jnp.bfloat16),
            jax.ShapeDtypeStruct((rows, rank), jnp.float32),
            jax.ShapeDtypeStruct((rows, 3 * rank), jnp.bfloat16),
        ],
        compiler_params=pltpu.CompilerParams(vmem_limit_bytes=VMEM_BYTES),
        cost_estimate=pl.CostEstimate(
            flops=4 * rows * tokens * rank, bytes_accessed=4 * rows * tokens, transcendentals=0
        ),
    )(starts, *arrays, test_parts)


def slab(rows_all, grads, sketch_split, test_high, test_low, core_map, first, block, columns, before):
    rows, tokens = rows_all.shape
    width = grads.shape[1]
    rank, rank_z = core_map.shape
    tile = largest_tile(rows, 768)
    turns = rows // tile
    at = first // block

    def kernel(rows_ref, grads_ref, split_ref, high_ref, low_ref, map_ref, *refs):
        corange_ref, residual_ref, project_ref, tiles_ref, sems = refs[-5:]
        step = pl.program_id(0) * turns + pl.program_id(1)
        slot = lax.rem(step, 2)

        def fetch(at_step):
            tile_at = pl.multiple_of(lax.rem(at_step, turns) * tile, tile)
            to = lax.rem(at_step, 2)
            return pltpu.make_async_copy(
                rows_ref.at[pl.ds(tile_at, tile), :], tiles_ref.at[to], sems.at[to]
            )

        @pl.when(step == 0)
        def _():
            fetch(step).start()

        @pl.when(pl.program_id(1) == 0)
        def _():
            corange = jnp.dot(high_ref[...], grads_ref[...], preferred_element_type=jnp.float32)
            corange += jnp.dot(low_ref[...], grads_ref[...], preferred_element_type=jnp.float32)
            corange_ref[...] = corange
            project = -jnp.dot(
                map_ref[...], corange, precision=highest, preferred_element_type=jnp.float32
            )
            high, low = split_two(project)
            project_ref[:rank, :] = high
            project_ref[rank : 2 * rank, :] = high
            project_ref[2 * rank :, :] = low

        fetch(step).wait()

        @pl.when(step + 1 < turns * (width // block))
        def _():
            fetch(step + 1).start()

        residual_ref[...] = jnp.dot(
            tiles_ref[slot], grads_ref[...], preferred_element_type=jnp.float32
        ) + jnp.dot(split_ref[...], project_ref[...], preferred_element_type=jnp.float32)

    in_specs = [
        pl.BlockSpec(memory_space=pl.ANY),
        pl.BlockSpec((tokens, block), lambda j, i: (0, j)),
        pl.BlockSpec((tile, 3 * rank), lambda j, i: (i, 0)),
        pl.BlockSpec((rank_z, tokens), lambda j, i: (0, 0)),
        pl.BlockSpec((rank_z, tokens), lambda j, i: (0, 0)),
        pl.BlockSpec((rank, rank_z), lambda j, i: (0, 0)),
    ] + [pl.BlockSpec(memory_space=pl.ANY)] * len(before)
    return pl.pallas_call(
        kernel,
        grid=(width // block, rows // tile),
        in_specs=in_specs,
        out_specs=[
            pl.BlockSpec((rank_z, block), lambda j, i: (0, at + j)),
            pl.BlockSpec((tile, block), lambda j, i: (i, at + j)),
        ],
        out_shape=[
            jax.ShapeDtypeStruct((rank_z, columns), jnp.float32),
            jax.ShapeDtypeStruct((rows, columns), jnp.float32),
        ],
        scratch_shapes=[
            pltpu.VMEM((3 * rank, block), jnp.bfloat16),
            pltpu.VMEM((2, tile, tokens), jnp.bfloat16),
            pltpu.SemaphoreType.DMA((2,)),
        ],
        input_output_aliases={6: 0, 7: 1} if before else {},
        compiler_params=pltpu.CompilerParams(vmem_limit_bytes=VMEM_BYTES),
        cost_estimate=pl.CostEstimate(
            flops=2 * width * (rows * (tokens + 3 * rank) + 2 * rank_z * tokens),
            bytes_accessed=4 * rows * width + 2 * tokens * (rows + width),
            transcendentals=0,
        ),
    )(rows_all, grads, sketch_split, test_high, test_low, core_map, *before)


def slices_of(columns):
    unit = largest_tile(columns, 512)
    count = columns // unit
    last = max(1, count // 9)
    middle = max(1, 2 * count // 9)
    slices, first = [], 0
    for n in (count - middle - last, middle, last):
        if n > 0:
            twice = n % 2 == 0 and first % (2 * unit) == 0
            slices.append((first, n * unit, 2 * unit if twice else unit))
            first += n * unit
    return slices


def solution(mesh):
    size_row, size_col = mesh.shape["row"], mesh.shape["col"]
    size_b = next(n for n in range(math.isqrt(size_col), size_col + 1) if size_col % n == 0)
    size_a = size_col // size_b
    size_core = 2 if size_row % 2 == 0 else 1
    size_z = size_row // size_core
    finer = Mesh(mesh.devices.reshape(size_z, size_core, size_a, size_b), ROW + COL)

    def per_device(inputs, out_grads, range_test, corange_test):
        z, core = lax.axis_index("z"), lax.axis_index("core")
        a, b = lax.axis_index("a"), lax.axis_index("b")
        col = a * size_b + b
        columns = out_grads.shape[1]
        rank, rank_z = range_test.shape[1], corange_test.shape[0]

        gathered = []
        for first, width, block in slices_of(columns):
            part = out_grads[:, first : first + width]
            gathered.append((first, block, lax.all_gather(part, ROW, axis=0, tiled=True)))

        grads_range = exact_product(out_grads.astype(jnp.float32), range_test, ((1,), (0,)))
        test_inputs = exact_product(inputs.astype(jnp.float32), corange_test, ((1,), (1,)))
        tokens = inputs.shape[0] * size_col
        unit = inputs.shape[0] // size_row
        range_terms = scattered(grads_range.reshape(size_col, unit, rank), COL, size_col, col)
        halves = turn(inputs, range_terms)
        rounds, starts = gather_tokens(halves, (size_a, size_b), (a, b))
        test_inputs = test_inputs.reshape(size_z, size_core, unit, rank_z).transpose(1, 0, 2, 3)
        test_inputs = sum(scattered(test_inputs, "core", size_core, core))
        test_terms = scattered(test_inputs, "z", size_z, z)
        own = combine(range_terms, test_terms, rounds[0])
        own = below([own] + [shifted(own, "z", size_z, by) for by in range(1, size_z)], rounds[1])
        own = gathered_parts(own, COL, size_col)
        stacks = [own] + [shifted(own, "core", size_core, by) for by in range(1, size_core)]
        at_core = lax.rem(core - jnp.arange(size_core) + size_core, size_core)[:, None, None]
        at_col = lax.rem(col - jnp.arange(size_col) + size_col, size_col)[None, :, None]
        at_z = lax.rem(z - jnp.arange(size_z) + size_z, size_z)[None, None, :]
        at_row = at_z * size_core + at_core
        range_starts = (at_row * size_col + at_col) * unit
        test_starts = (at_col * size_row + at_row) * unit
        range_parts, test_high, test_low, core_input = finish(
            stacks,
            range_starts.reshape(-1).astype(jnp.int32),
            test_starts.reshape(-1).astype(jnp.int32),
            rank,
        )

        gram_matrix = exact_product(core_input, core_input, ((0,), (0,)))
        factor_low = jnp.linalg.cholesky(gram_matrix)
        core_map = jax.scipy.linalg.cho_solve((factor_low, True), core_input.T)

        rows_all, new_range, sketch_split = assemble(sum(rounds, []), starts, range_parts)

        out = ()
        for first, block, grads in gathered:
            out = slab(
                rows_all, grads, sketch_split, test_high, test_low, core_map, first, block, columns, out
            )
        return (new_range, out[0], out[1])

    return jax.shard_map(
        per_device,
        mesh=finer,
        in_specs=(P(COL, ROW), P(ROW, COL), P(COL, None), P(None, ROW)),
        out_specs=(P(ROW, None), P(None, COL), P(ROW, COL)),
        check_vma=False,
    )
```
